512 devices in a mesh: row: 16 (over z), col: 32 (over x, y, core).
Axes of the slice: x: 4, y: 4, z: 16, core: 2. Of those that a mesh axis runs over, the one named last changes fastest.
Arguments:
- level_one: bfloat16 [192, 262144], P(None, ('row', 'col')), may hold values from -6 to 6
- child_maps: bfloat16 [8, 192, 192], replicated, may hold values from -0.15625 to 0.15625
- translations: bfloat16 [32, 192, 192], replicated, may hold values from -0.078125 to 0.078125
- send_one: int32 [512, 32, 32], P(('row', 'col')), may hold values from 0 to 511
- list_one: int32 [262144, 32], P(('row', 'col')), may hold values from -1 to 1535, as said below
- send_two: int32 [512, 16, 16], P(('row', 'col')), may hold values from 0 to 63
- list_two: int32 [32768, 32], P(('row', 'col')), may hold values from -1 to 319, as said below
- list_three: int32 [4096, 32], P(('row', 'col')), may hold values from -1 to 255, as said below
Outputs:
- local_one: float32 [192, 262144], P(None, ('row', 'col'))
- local_two: float32 [192, 32768], P(None, ('row', 'col'))
- local_three: float32 [192, 4096], P(None, ('row', 'col'))
The draws below stay inside these ranges and needn't reach their ends.
Inputs may be any that keep to these rules, and one draw needn't show every extreme that they name: `list_one`: -1 marks an offset without a source box. `list_two`: -1 marks an offset without a source box. `list_three`: -1 marks an offset without a source box.
All inputs are finite; a program needn't handle non-finite values.
Results may differ from the reference program's by a relative error of at most 0.0041.
Values may be sent and summed in bfloat16 or wider, within the bound.
A program may use at most 64 MiB of HBM per device.

```python
import jax
import jax.numpy as jnp
from jax import lax

D = 192
NOFF = 32
B1_DEV = 512
B2_DEV = 64
GH1 = 32
GH2 = 16
SEG3 = 256
BUF1 = 1536
BUF2 = 320
N1 = 262144
N2 = 32768
N3 = 4096
N_ROW = 16
N_COL = 32


def sparse_list(key, count, limit):
    slot_key, keep_key = jax.random.split(key)
    slots = jax.random.randint(slot_key, (count, NOFF), 0, limit, dtype=jnp.int32)
    keeper = jax.random.randint(keep_key, (count, NOFF), 0, 20, dtype=jnp.int32)
    return jnp.where(keeper >= 3, slots, -1).astype(jnp.int32)


def draw_list_one(key, part):
    key = jax.random.fold_in(key, 11)
    return sparse_list(key, N1, BUF1)


def draw_list_two(key, part):
    key = jax.random.fold_in(key, 23)
    return sparse_list(key, N2, BUF2)


def draw_list_three(key, part):
    key = jax.random.fold_in(key, 37)
    return sparse_list(key, N3, SEG3)


def place_ends(result, stream_key, low, high):
    index_at = [jax.random.randint(jax.random.fold_in(stream_key, axis), (), 0, length) for axis, length in enumerate(result.shape)]
    widest = result.shape.index(max(result.shape))
    beside = index_at[:widest] + [(index_at[widest] + 1) % result.shape[widest]] + index_at[widest + 1:]
    return result.at[tuple(index_at)].set(low).at[tuple(beside)].set(high)


def levels(own_key, extent, pieces, low, largest):
    loudness, own = 1.0, jax.random.fold_in(own_key, 6)
    for position, parts in pieces:
        heights = jnp.exp(jax.random.uniform(jax.random.fold_in(own, position), (parts,), jnp.float32, low / len(pieces), largest / len(pieces)))
        loudness = loudness * jnp.repeat(heights, extent[position] // parts).reshape([-1 if axis == position else 1 for axis in range(len(extent))])
    return loudness


def normal_values(key, shape, spread, bound, cuts=(), kind=jnp.bfloat16):
    result = jax.random.normal(key, shape, jnp.float32) * spread
    if len(cuts) > 0:
        result = levels(key, shape, cuts, -0.22, 0.18) * result
    return jnp.clip(result, min=-bound, max=bound).astype(kind)


def setup_inputs(seed: int = 0) -> dict:
    arg_keys = jax.random.split(jax.random.key(seed), 9)
    level_one = normal_values(arg_keys[0], (D, N1), 1.0, 6.0, ((1, 512),))
    child_maps = normal_values(arg_keys[1], (8, D, D), (8 * D) ** -0.5, 0.15625)
    translations = normal_values(arg_keys[2], (NOFF, D, D), (D * NOFF) ** -0.5, 0.078125)
    send_one = place_ends(jax.random.randint(arg_keys[3], (N_ROW * N_COL, N_COL, GH1), 0, B1_DEV), jax.random.fold_in(arg_keys[3], 1), 0, B1_DEV - 1).astype(jnp.int32)
    list_one = draw_list_one(jax.random.fold_in(arg_keys[8], 71), 0)
    send_two = place_ends(jax.random.randint(arg_keys[5], (N_ROW * N_COL, N_ROW, GH2), 0, B2_DEV), jax.random.fold_in(arg_keys[5], 1), 0, B2_DEV - 1).astype(jnp.int32)
    list_two = draw_list_two(jax.random.fold_in(arg_keys[8], 71), 0)
    list_three = draw_list_three(jax.random.fold_in(arg_keys[8], 71), 0)
    return {"level_one": level_one, "child_maps": child_maps, "translations": translations, "send_one": send_one, "list_one": list_one, "send_two": send_two, "list_two": list_two, "list_three": list_three}


def ascend(children, child_ops):
    parents = children.shape[1] // 8
    grouped = children.reshape(children.shape[0], parents, 8).astype(jnp.float32)
    summed = jnp.einsum('cde,ebc->db', child_ops.astype(jnp.float32), grouped)
    return summed.astype(jnp.bfloat16)


def translate(buffer, entries, operators):
    clipped = jnp.maximum(entries, 0).astype(jnp.int32)
    columns = jnp.take(buffer, clipped.T, axis=1)
    columns = jnp.where((entries >= 0).T[None], columns, jnp.zeros_like(columns))
    return jnp.einsum('ode,eob->db', operators.astype(jnp.float32), columns.astype(jnp.float32))


def reference(level_one, child_maps, translations, send_one, list_one, send_two, list_two, list_three):
    parents_two = ascend(level_one, child_maps)
    parents_three = ascend(parents_two, child_maps)
    width = level_one.shape[0]

    def first_level(device):
        row_id = device // N_COL
        col_id = device % N_COL
        own_part = lax.dynamic_slice_in_dim(level_one, device * B1_DEV, B1_DEV, 1)
        peer_ids = row_id * N_COL + jnp.arange(N_COL, dtype=jnp.int32)
        local_ids = send_one[peer_ids, col_id, :]
        global_ids = (peer_ids[:, None] * B1_DEV + local_ids).reshape(-1).astype(jnp.int32)
        buffer = jnp.concatenate([own_part, jnp.take(level_one, global_ids, axis=1)], axis=1)
        entries = lax.dynamic_slice_in_dim(list_one, device * B1_DEV, B1_DEV, 0)
        return translate(buffer, entries, translations)

    def second_level(device):
        row_id = device // N_COL
        col_id = device % N_COL
        own_part = lax.dynamic_slice_in_dim(parents_two, device * B2_DEV, B2_DEV, 1)
        peer_ids = jnp.arange(N_ROW, dtype=jnp.int32) * N_COL + col_id
        local_ids = send_two[peer_ids, row_id, :]
        global_ids = (peer_ids[:, None] * B2_DEV + local_ids).reshape(-1).astype(jnp.int32)
        buffer = jnp.concatenate([own_part, jnp.take(parents_two, global_ids, axis=1)], axis=1)
        entries = lax.dynamic_slice_in_dim(list_two, device * B2_DEV, B2_DEV, 0)
        return 0.5 * translate(buffer, entries, translations)

    def third_level(row_id):
        segment = lax.dynamic_slice_in_dim(parents_three, row_id * SEG3, SEG3, 1)
        entries = lax.dynamic_slice_in_dim(list_three, row_id * SEG3, SEG3, 0)
        return 0.25 * translate(segment, entries, translations)

    devices = jnp.arange(N_ROW * N_COL, dtype=jnp.int32)
    local_one = lax.map(first_level, devices)
    local_one = jnp.transpose(local_one, (1, 0, 2)).reshape(width, N1)
    local_two = lax.map(second_level, devices)
    local_two = jnp.transpose(local_two, (1, 0, 2)).reshape(width, N2)
    local_three = lax.map(third_level, jnp.arange(N_ROW, dtype=jnp.int32))
    local_three = jnp.transpose(local_three, (1, 0, 2)).reshape(width, N3)
    return (local_one, local_two, local_three)
```

```python
import jax
import jax.numpy as jnp
from jax import lax
from jax.experimental import pallas as pl
from jax.experimental.pallas import tpu as pltpu
from jax.sharding import PartitionSpec as P

BF = jnp.bfloat16
F32 = jnp.float32
NT = (((1,), (1,)), ((), ()))
D, NOFF, B1, B2, B3 = 192, 32, 512, 64, 8
NCOL, NROW, GH1, GH2 = 32, 16, 32, 16
MESH = pl.DeviceIdType.MESH


def iota(shape, axis):
    return lax.broadcasted_iota(jnp.int32, shape, axis)


def dot(a, b):
    return jnp.dot(a, b, preferred_element_type=F32)


def dot_nt(a, b):
    return lax.dot_general(a, b, NT, preferred_element_type=F32)


def hot(mask):
    return jnp.where(mask, 1.0, 0.0).astype(BF)


def turned(table):
    eye = hot(iota((D, D), 0) == iota((D, D), 1))
    return dot_nt(eye, table).astype(BF)


def kernel(
    one_ref, send1_ref, list1_ref, send2_ref, list2_ref, list3_ref, maps_hbm, trans_hbm,
    out1_ref, out2_ref, out3_ref,
    maps, trans, tcat, send1, ghost1, send2, ghost2, send3, ghost3, g1, g23, tab1,
    load_sem, send_sem, recv_sem,
):
    row = lax.axis_index("row")
    col = lax.axis_index("col")
    load_maps = pltpu.make_async_copy(maps_hbm, maps, load_sem.at[0])
    load_trans = pltpu.make_async_copy(trans_hbm, trans, load_sem.at[1])
    load_maps.start()
    load_trans.start()

    barrier = pltpu.get_barrier_semaphore()

    def hello_col(i, _):
        pl.semaphore_signal(barrier, inc=1, device_id=(row, (col + i) % NCOL), device_id_type=MESH)
        return 0

    def hello_row(i, _):
        pl.semaphore_signal(barrier, inc=1, device_id=((row + i) % NROW, col), device_id_type=MESH)
        return 0

    lax.fori_loop(1, NCOL, hello_col, 0)
    lax.fori_loop(1, NROW, hello_row, 0)

    who = send1_ref[...].T
    lane = iota((GH1, B1), 1)
    for p0 in range(0, NCOL, 8):
        pick = jnp.concatenate([hot(who[:, p : p + 1] == lane) for p in range(p0, p0 + 8)], axis=0)
        rows = dot_nt(pick, one_ref[...]).astype(BF)
        send1[p0 : p0 + 8] = rows.reshape(8, GH1, D)
    ghost1[col] = send1[col]

    pl.semaphore_wait(barrier, NCOL - 1 + NROW - 1)

    def to_col1(i):
        peer = (col + i) % NCOL
        return pltpu.make_async_remote_copy(
            src_ref=send1.at[peer], dst_ref=ghost1.at[col], send_sem=send_sem.at[0],
            recv_sem=recv_sem.at[0], device_id=(row, peer), device_id_type=MESH)

    def to_row2(i):
        peer = (row + i) % NROW
        return pltpu.make_async_remote_copy(
            src_ref=send2.at[peer], dst_ref=ghost2.at[row], send_sem=send_sem.at[1],
            recv_sem=recv_sem.at[1], device_id=(peer, col), device_id_type=MESH)

    def to_col3(i):
        peer = (col + i) % NCOL
        return pltpu.make_async_remote_copy(
            src_ref=send3, dst_ref=ghost3.at[col], send_sem=send_sem.at[2],
            recv_sem=recv_sem.at[2], device_id=(row, peer), device_id_type=MESH)

    def start(copy):
        def step(i, _):
            copy(i).start()
            return 0
        return step

    lax.fori_loop(1, NCOL, start(to_col1), 0)

    load_maps.wait()
    r = iota((B1, B1), 0)
    pick = hot(iota((B1, B1), 1) == (r & (B2 - 1)) * 8 + (r >> 6))
    children = dot_nt(pick, one_ref[...]).astype(BF)
    total = jnp.zeros((B2, D), F32)
    for c in range(8):
        total = total + dot_nt(children[c * B2 : (c + 1) * B2], maps[c])
    two = total.astype(BF)
    who = send2_ref[...].T
    lane = iota((GH2, B2), 1)
    pick = jnp.concatenate([hot(who[:, p : p + 1] == lane) for p in range(NROW)], axis=0)
    send2[...] = dot(pick, two).astype(BF).reshape(NROW, GH2, D)
    ghost2[row] = send2[row]
    lax.fori_loop(1, NROW, start(to_row2), 0)

    r = iota((128, B2), 0)
    pick = hot(iota((128, B2), 1) == (r & 15) * 8 + (r >> 4))
    children = dot(pick, two).astype(BF)
    total = jnp.zeros((16, D), F32)
    for c in range(8):
        total = total + dot_nt(children[c * 16 : (c + 1) * 16], maps[c])
    three = total.astype(BF)
    send3[...] = three
    ghost3[col] = three
    lax.fori_loop(1, NCOL, start(to_col3), 0)

    def own(o, _):
        pick = hot(iota((B1, B1), 0) == list1_ref[pl.ds(o, 1), :])
        g1[pl.ds(pl.multiple_of(o * D, D), D), :] = dot(one_ref[...], pick).astype(BF)
        return 0

    lax.fori_loop(0, NOFF, own, 0, unroll=2)

    load_trans.wait()
    for o in range(0, NOFF, 2):
        tcat[:, o * D : (o + 2) * D] = jnp.concatenate([trans[o], trans[o + 1]], axis=1)

    pltpu.make_async_copy(ghost1.at[0 : NCOL - 1], ghost1.at[0 : NCOL - 1], recv_sem.at[0]).wait()
    tab1[...] = turned(ghost1[...].reshape(NCOL * GH1, D))

    def far(o, _):
        pick = hot(iota((NCOL * GH1, B1), 0) == list1_ref[pl.ds(o, 1), :] - B1)
        at = pl.ds(pl.multiple_of(o * D, D), D)
        g1[at, :] = g1[at, :] + dot(tab1[...], pick).astype(BF)
        return 0

    lax.fori_loop(0, NOFF, far, 0, unroll=2)
    out1_ref[...] = dot(tcat[...], g1[...])

    pltpu.make_async_copy(ghost2.at[0 : NROW - 1], ghost2.at[0 : NROW - 1], recv_sem.at[1]).wait()
    tab2 = turned(jnp.concatenate([two, ghost2[...].reshape(NROW * GH2, D)], axis=0))
    list2 = list2_ref[...]
    g23[...] = jnp.zeros_like(g23)
    for o in range(0, NOFF, 4):
        entries = jnp.concatenate([list2[o + j : o + j + 1, :] for j in range(4)], axis=1)
        pick = hot(iota((B2 + NROW * GH2, 4 * B2), 0) == entries)
        found = dot(tab2, pick).astype(BF)
        for j in range(4):
            g23[(o + j) * D : (o + j + 1) * D, 0:B2] = found[:, j * B2 : (j + 1) * B2]

    pltpu.make_async_copy(ghost3.at[0 : NCOL - 1], ghost3.at[0 : NCOL - 1], recv_sem.at[2]).wait()
    tab3 = turned(ghost3[...].reshape(NCOL * 16, D))
    spread = hot(iota((NOFF, NOFF * B3), 1) // B3 == iota((NOFF, NOFF * B3), 0))
    wide = dot(list3_ref[...].astype(F32).astype(BF), spread)
    keep = iota((B3, NOFF * B3), 1) % B3 == iota((B3, NOFF * B3), 0)
    entries = jnp.sum(jnp.where(keep, wide, 0.0), axis=0, keepdims=True).astype(jnp.int32)
    entries = entries + (entries & -8)
    pick = hot(iota((NCOL * 16, NOFF * B3), 0) == entries)
    found = dot(tab3, pick).astype(BF)
    for o in range(NOFF):
        g23[o * D : (o + 1) * D, B2 : B2 + B3] = found[:, o * B3 : (o + 1) * B3]
    both = dot(tcat[...], g23[...])
    both = both.T
    out2_ref[...] = 0.5 * both[0:B2]
    out3_ref[...] = 0.25 * both[B2 : B2 + B3]

    pltpu.make_async_copy(send1.at[0 : NCOL - 1], send1.at[0 : NCOL - 1], send_sem.at[0]).wait()
    pltpu.make_async_copy(send2.at[0 : NROW - 1], send2.at[0 : NROW - 1], send_sem.at[1]).wait()
    pltpu.make_async_copy(ghost3.at[0 : NCOL - 1], ghost3.at[0 : NCOL - 1], send_sem.at[2]).wait()


def on_device(
    level_one, child_maps, translations, send_one, list_one, send_two, list_two, list_three
):
    vmem = pl.BlockSpec(memory_space=pltpu.VMEM)
    any_ = pl.BlockSpec(memory_space=pl.ANY)
    out1, out2, out3 = pl.pallas_call(
        kernel,
        out_shape=(
            jax.ShapeDtypeStruct((D, B1), F32),
            jax.ShapeDtypeStruct((B2, D), F32),
            jax.ShapeDtypeStruct((B3, D), F32),
        ),
        in_specs=[vmem] * 6 + [any_] * 2,
        out_specs=(vmem, vmem, vmem),
        scratch_shapes=[
            pltpu.VMEM((8, D, D), BF),
            pltpu.VMEM((NOFF, D, D), BF),
            pltpu.VMEM((D, NOFF * D), BF),
            pltpu.VMEM((NCOL, GH1, D), BF),
            pltpu.VMEM((NCOL, GH1, D), BF),
            pltpu.VMEM((NROW, GH2, D), BF),
            pltpu.VMEM((NROW, GH2, D), BF),
            pltpu.VMEM((16, D), BF),
            pltpu.VMEM((NCOL, 16, D), BF),
            pltpu.VMEM((NOFF * D, B1), BF),
            pltpu.VMEM((NOFF * D, 128), BF),
            pltpu.VMEM((D, NCOL * GH1), BF),
            pltpu.SemaphoreType.DMA((2,)),
            pltpu.SemaphoreType.DMA((3,)),
            pltpu.SemaphoreType.DMA((3,)),
        ],
        compiler_params=pltpu.CompilerParams(
            collective_id=0, has_side_effects=True, vmem_limit_bytes=60 << 20
        ),
    )(
        level_one, send_one.reshape(NCOL, GH1), list_one.T, send_two.reshape(NROW, GH2),
        list_two.T, list_three, child_maps, translations,
    )
    return out1, out2.T, out3.T


def solution(mesh):
    placed = (
        P(None, ("row", "col")),
        P(),
        P(),
        P(("row", "col"), None, None),
        P(("row", "col"), None),
        P(("row", "col"), None, None),
        P(("row", "col"), None),
        P(("row", "col"), None),
    )
    return jax.shard_map(
        on_device,
        mesh=mesh,
        in_specs=placed,
        out_specs=(P(None, ("row", "col")), P(None, ("row", "col")), P(None, ("row", "col"))),
        check_vma=False,
    )
```

```python
import jax
import jax.numpy as jnp
from jax import lax
from jax.experimental import pallas as pl
from jax.experimental.pallas import tpu as pltpu
from jax.sharding import PartitionSpec as P

BF = jnp.bfloat16
F32 = jnp.float32
NT = (((1,), (1,)), ((), ()))
D, NOFF, B1, B2, B3 = 192, 32, 512, 64, 8
NCOL, NROW, GH1, GH2 = 32, 16, 32, 16
ROWS = B2 + NROW
SLAB, WIDE = 128, 256
MESH = pl.DeviceIdType.MESH


def iota(shape, axis):
    return lax.broadcasted_iota(jnp.int32, shape, axis)


def dot(a, b):
    return jnp.dot(a, b, preferred_element_type=F32)


def dot_nt(a, b):
    return lax.dot_general(a, b, NT, preferred_element_type=F32)


def hot(mask):
    return jnp.where(mask, 1.0, 0.0).astype(BF)


def turned(table):
    eye = hot(iota((D, D), 0) == iota((D, D), 1))
    return dot_nt(eye, table).astype(BF)


def upward(one_ref, maps, send2_ref, table_ref, three_ref):
    r = iota((B1, B1), 0)
    pick = hot(iota((B1, B1), 1) == (r & (B2 - 1)) * 8 + (r >> 6))
    children = dot_nt(pick, one_ref[...]).astype(BF)
    total = jnp.zeros((B2, D), F32)
    for c in range(8):
        total = total + dot_nt(children[c * B2 : (c + 1) * B2], maps[c])
    two = total.astype(BF)
    table_ref[...] = jnp.zeros_like(table_ref)
    table_ref[0:B2, 0:D] = two
    spread = hot(iota((NROW, D), 0) == iota((NROW, D), 1))
    table_ref[B2:ROWS, 0:D] = dot(send2_ref[...].astype(F32).astype(BF), spread).astype(BF)
    r = iota((128, B2), 0)
    pick = hot(iota((128, B2), 1) == (r & 15) * 8 + (r >> 4))
    children = dot(pick, two).astype(BF)
    total = jnp.zeros((16, D), F32)
    for c in range(8):
        total = total + dot_nt(children[c * 16 : (c + 1) * 16], maps[c])
    three_ref[...] = total.astype(BF)


def plane(
    one_hbm, send1_ref, list1_hbm, list3_ref, three_ref, trans_hbm,
    out1_ref, out3_ref,
    one_ref, list1_ref, trans, tcat, send1, ghost1, ghost3, g1, g3, tab1,
    load_sem, send_sem, recv_sem,
):
    row = lax.axis_index("row")
    col = lax.axis_index("col")
    load_one = pltpu.make_async_copy(one_hbm, one_ref, load_sem.at[0])
    load_list = pltpu.make_async_copy(list1_hbm, list1_ref, load_sem.at[1])
    load_trans = pltpu.make_async_copy(trans_hbm, trans, load_sem.at[2])
    load_one.start()
    load_list.start()
    load_trans.start()

    barrier = pltpu.get_barrier_semaphore()

    def hello(i, _):
        pl.semaphore_signal(barrier, inc=1, device_id=(row, (col + i) % NCOL), device_id_type=MESH)
        return 0

    lax.fori_loop(1, NCOL, hello, 0)

    who = send1_ref[...].T
    lane = iota((GH1, B1), 1)
    load_one.wait()
    for p0 in range(0, NCOL, 8):
        pick = jnp.concatenate([hot(who[:, p : p + 1] == lane) for p in range(p0, p0 + 8)], axis=0)
        rows = dot_nt(pick, one_ref[...]).astype(BF)
        send1[p0 : p0 + 8] = rows.reshape(8, GH1, D)
    ghost1[col] = send1[col]
    ghost3[col] = three_ref[...]

    pl.semaphore_wait(barrier, NCOL - 1)

    def to_col1(i):
        peer = (col + i) % NCOL
        return pltpu.make_async_remote_copy(
            src_ref=send1.at[peer], dst_ref=ghost1.at[col], send_sem=send_sem.at[0],
            recv_sem=recv_sem.at[0], device_id=(row, peer), device_id_type=MESH)

    def to_col3(i):
        peer = (col + i) % NCOL
        return pltpu.make_async_remote_copy(
            src_ref=three_ref, dst_ref=ghost3.at[col], send_sem=send_sem.at[1],
            recv_sem=recv_sem.at[1], device_id=(row, peer), device_id_type=MESH)

    def start(copy):
        def step(i, _):
            copy(i).start()
            return 0
        return step

    lax.fori_loop(1, NCOL, start(to_col1), 0)
    lax.fori_loop(1, NCOL, start(to_col3), 0)

    load_list.wait()

    def own(o, _):
        pick = hot(iota((B1, B1), 0) == list1_ref[pl.ds(o, 1), :])
        g1[pl.ds(pl.multiple_of(o * D, D), D), :] = dot(one_ref[...], pick).astype(BF)
        return 0

    lax.fori_loop(0, NOFF, own, 0, unroll=2)

    load_trans.wait()
    for o in range(0, NOFF, 2):
        tcat[:, o * D : (o + 2) * D] = jnp.concatenate([trans[o], trans[o + 1]], axis=1)

    pltpu.make_async_copy(ghost3.at[0 : NCOL - 1], ghost3.at[0 : NCOL - 1], recv_sem.at[1]).wait()
    tab3 = turned(ghost3[...].reshape(NCOL * 16, D))
    spread = hot(iota((NOFF, NOFF * B3), 1) // B3 == iota((NOFF, NOFF * B3), 0))
    wide = dot(list3_ref[...].astype(F32).astype(BF), spread)
    keep = iota((B3, NOFF * B3), 1) % B3 == iota((B3, NOFF * B3), 0)
    entries = jnp.sum(jnp.where(keep, wide, 0.0), axis=0, keepdims=True).astype(jnp.int32)
    entries = entries + (entries & -8)
    pick = hot(iota((NCOL * 16, NOFF * B3), 0) == entries)
    found = dot(tab3, pick).astype(BF)
    g3[...] = jnp.zeros_like(g3)
    for o in range(NOFF):
        g3[o * D : (o + 1) * D, 0:B3] = found[:, o * B3 : (o + 1) * B3]
    out3_ref[...] = 0.25 * dot(tcat[...], g3[...]).T[0:B3]

    pltpu.make_async_copy(ghost1.at[0 : NCOL - 1], ghost1.at[0 : NCOL - 1], recv_sem.at[0]).wait()
    tab1[...] = turned(ghost1[...].reshape(NCOL * GH1, D))

    def far(o, _):
        pick = hot(iota((NCOL * GH1, B1), 0) == list1_ref[pl.ds(o, 1), :] - B1)
        at = pl.ds(pl.multiple_of(o * D, D), D)
        g1[at, :] = g1[at, :] + dot(tab1[...], pick).astype(BF)
        return 0

    lax.fori_loop(0, NOFF, far, 0, unroll=2)
    out1_ref[...] = dot(tcat[...], g1[...])

    pltpu.make_async_copy(ghost1.at[0 : NCOL - 1], ghost1.at[0 : NCOL - 1], send_sem.at[0]).wait()
    pltpu.make_async_copy(ghost3.at[0 : NCOL - 1], ghost3.at[0 : NCOL - 1], send_sem.at[1]).wait()


def across(
    table_ref, list2_ref, out1_in, out3_in, trans_hbm, out1_ref, out2_ref, out3_ref, trans, sem,
):
    row = lax.axis_index("row")
    pass1 = pltpu.make_async_copy(out1_in, out1_ref, sem.at[0])
    load_trans = pltpu.make_async_copy(trans_hbm, trans, sem.at[1])
    load_trans.start()
    pass1.start()
    out3_ref[...] = out3_in[...]

    table = table_ref[:, 0:ROWS, 0:D].reshape(NROW * ROWS, D)
    every = turned(table)
    mine = hot(iota((NROW, NROW * ROWS), 1) == iota((NROW, NROW * ROWS), 0) * ROWS + B2 + row)
    sent = dot(mine, table)[:, 0:GH2].astype(BF)
    ghosts = NROW * GH2
    spread = hot(iota((NROW, ghosts), 1) // GH2 == iota((NROW, ghosts), 0))
    wide = lax.dot_general(sent, spread, (((0,), (0,)), ((), ())), preferred_element_type=F32)
    keep = iota((GH2, ghosts), 1) % GH2 == iota((GH2, ghosts), 0)
    local = jnp.sum(jnp.where(keep, wide, 0.0), axis=0, keepdims=True).astype(jnp.int32)
    source = local + iota((1, ghosts), 1) // GH2 * ROWS
    pick = hot(iota((NROW * ROWS, ghosts), 0) == source)
    far = dot(every, pick).astype(BF)
    pick = hot(iota((NROW * ROWS, B2), 0) == iota((NROW * ROWS, B2), 1) + row * ROWS)
    near = dot(every, pick).astype(BF)

    list2 = list2_ref[...]
    load_trans.wait()
    total = jnp.zeros((D, B2), F32)
    for o in range(0, NOFF, 4):
        entries = jnp.concatenate([list2[o + j : o + j + 1, :] for j in range(4)], axis=1)
        found = dot(near, hot(iota((B2, 4 * B2), 0) == entries))
        found = found + dot(far, hot(iota((ghosts, 4 * B2), 0) == entries - B2))
        found = found.astype(BF)
        for j in range(4):
            total = total + dot(trans[o + j], found[:, j * B2 : (j + 1) * B2])
    out2_ref[...] = 0.5 * total.T
    pass1.wait()


def on_device(
    level_one, child_maps, translations, send_one, list_one, send_two, list_two, list_three
):
    vmem = pl.BlockSpec(memory_space=pltpu.VMEM)
    any_ = pl.BlockSpec(memory_space=pl.ANY)
    table, three = pl.pallas_call(
        upward,
        out_shape=(jax.ShapeDtypeStruct((SLAB, WIDE), BF), jax.ShapeDtypeStruct((16, D), BF)),
        in_specs=[vmem] * 3,
        out_specs=(vmem, vmem),
    )(level_one, child_maps, send_two.reshape(NROW, GH2))
    tables = lax.all_gather(table, "row", axis=0, tiled=True)
    out1, out3 = pl.pallas_call(
        plane,
        out_shape=(jax.ShapeDtypeStruct((D, B1), F32), jax.ShapeDtypeStruct((B3, D), F32)),
        in_specs=[any_, vmem, any_, vmem, vmem, any_],
        out_specs=(vmem, vmem),
        scratch_shapes=[
            pltpu.VMEM((D, B1), BF),
            pltpu.VMEM((NOFF, B1), jnp.int32),
            pltpu.VMEM((NOFF, D, D), BF),
            pltpu.VMEM((D, NOFF * D), BF),
            pltpu.VMEM((NCOL, GH1, D), BF),
            pltpu.VMEM((NCOL, GH1, D), BF),
            pltpu.VMEM((NCOL, 16, D), BF),
            pltpu.VMEM((NOFF * D, B1), BF),
            pltpu.VMEM((NOFF * D, 128), BF),
            pltpu.VMEM((D, NCOL * GH1), BF),
            pltpu.SemaphoreType.DMA((3,)),
            pltpu.SemaphoreType.DMA((2,)),
            pltpu.SemaphoreType.DMA((2,)),
        ],
        compiler_params=pltpu.CompilerParams(
            collective_id=0, has_side_effects=True, vmem_limit_bytes=60 << 20
        ),
        cost_estimate=pl.CostEstimate(
            flops=2 * NOFF * D * B1 * (3 * B1 + D), bytes_accessed=4 << 20, transcendentals=0
        ),
    )(
        level_one, send_one.reshape(NCOL, GH1), list_one.T, list_three, three, translations,
    )
    out1, out2, out3 = pl.pallas_call(
        across,
        out_shape=(
            jax.ShapeDtypeStruct((D, B1), F32),
            jax.ShapeDtypeStruct((B2, D), F32),
            jax.ShapeDtypeStruct((B3, D), F32),
        ),
        in_specs=[vmem, vmem, any_, vmem, any_],
        out_specs=(any_, vmem, vmem),
        scratch_shapes=[pltpu.VMEM((NOFF, D, D), BF), pltpu.SemaphoreType.DMA((2,))],
        compiler_params=pltpu.CompilerParams(vmem_limit_bytes=60 << 20),
    )(tables.reshape(NROW, SLAB, WIDE), list_two.T, out1, out3, translations)
    return out1, out2.T, out3.T


def solution(mesh):
    placed = (
        P(None, ("row", "col")),
        P(),
        P(),
        P(("row", "col"), None, None),
        P(("row", "col"), None),
        P(("row", "col"), None, None),
        P(("row", "col"), None),
        P(("row", "col"), None),
    )
    return jax.shard_map(
        on_device,
        mesh=mesh,
        in_specs=placed,
        out_specs=(P(None, ("row", "col")), P(None, ("row", "col")), P(None, ("row", "col"))),
        check_vma=False,
    )
```

```python
import jax
import jax.numpy as jnp
from jax import lax
from jax.experimental import pallas as pl
from jax.experimental.pallas import tpu as pltpu
from jax.sharding import PartitionSpec as P

BF = jnp.bfloat16
F32 = jnp.float32
NT = (((1,), (1,)), ((), ()))
D, NOFF, B1, B2, B3 = 192, 32, 512, 64, 8
NCOL, NROW, GH1, GH2 = 32, 16, 32, 16
PACK = 48
MESSAGE = PACK + 2 * B3
MESH = pl.DeviceIdType.MESH


def iota(shape, axis):
    return lax.broadcasted_iota(jnp.int32, shape, axis)


def dot(a, b):
    return jnp.dot(a, b, preferred_element_type=F32)


def dot_nt(a, b):
    return lax.dot_general(a, b, NT, preferred_element_type=F32)


def hot(mask):
    return jnp.where(mask, 1.0, 0.0).astype(BF)


def turned(table):
    w = table.shape[1]
    eye = hot(iota((w, w), 0) == iota((w, w), 1))
    return dot_nt(eye, table).astype(BF)


def as_row(entries, width):
    k, p = entries.shape
    n = p * width
    spread = hot(iota((p, n), 1) // width == iota((p, n), 0))
    wide = dot(entries.astype(F32).astype(BF), spread)
    keep = iota((k, n), 1) % width == iota((k, n), 0)
    return jnp.sum(jnp.where(keep, wide, 0.0), axis=0, keepdims=True).astype(jnp.int32)


def kernel(
    one_hbm, send1_ref, list1_hbm, send2_ref, list2_ref, list3_ref, maps_hbm, trans_hbm,
    out1_ref, out2_ref, out3_ref,
    one_ref, list1_ref, maps, trans, tcat, send1, ghost1, send2, ghost2, g, tab1,
    load_sem, send_sem, recv_sem,
):
    row = lax.axis_index("row")
    col = lax.axis_index("col")
    barrier = pltpu.get_barrier_semaphore()

    def hello_col(i, _):
        pl.semaphore_signal(barrier, inc=1, device_id=(row, lax.rem(col + i, NCOL)), device_id_type=MESH)
        return 0

    def hello_row(i, _):
        pl.semaphore_signal(barrier, inc=1, device_id=(lax.rem(row + i, NROW), col), device_id_type=MESH)
        return 0

    load_one = pltpu.make_async_copy(one_hbm, one_ref, load_sem.at[0])
    load_one.start()
    load_maps = pltpu.make_async_copy(maps_hbm, maps, load_sem.at[1])
    load_maps.start()
    lax.fori_loop(1, NROW, hello_row, 0)
    lax.fori_loop(1, NCOL, hello_col, 0)
    load_list = pltpu.make_async_copy(list1_hbm, list1_ref, load_sem.at[2])
    load_trans = pltpu.make_async_copy(trans_hbm, trans, load_sem.at[3])
    load_list.start()
    load_trans.start()

    who = send1_ref[...].T
    lane = iota((GH1, B1), 1)
    load_one.wait()
    for p0 in range(0, NCOL, 8):
        pick = jnp.concatenate([hot(who[:, p : p + 1] == lane) for p in range(p0, p0 + 8)], axis=0)
        rows = dot_nt(pick, one_ref[...]).reshape(8, GH1, D)
        send1[p0 : p0 + 8, 0:GH1] = rows[:, :, 0:128].astype(BF)
        rest = rows[:, :, 128:D]
        rest = jnp.concatenate([rest[:, 0 : GH1 // 2], rest[:, GH1 // 2 :]], axis=2)
        send1[p0 : p0 + 8, GH1:PACK] = rest.astype(BF)
    load_maps.wait()
    r = iota((B1, B1), 0)
    pick = hot(iota((B1, B1), 1) == (r & (B2 - 1)) * 8 + (r >> 6))
    children = dot_nt(pick, one_ref[...]).astype(BF)
    total = jnp.zeros((B2, D), F32)
    for c in range(8):
        total = total + dot_nt(children[c * B2 : (c + 1) * B2], maps[c])
    two = total.astype(BF)
    who = send2_ref[...].T
    lane = iota((GH2, B2), 1)
    pick = jnp.concatenate([hot(who[:, p : p + 1] == lane) for p in range(NROW)], axis=0)
    send2[...] = dot(pick, two).astype(BF).reshape(NROW, GH2, D)
    ghost2[row] = send2[row]

    r = iota((128, B2), 0)
    pick = hot(iota((128, B2), 1) == (r & 15) * 8 + (r >> 4))
    children = dot(pick, two).astype(BF)
    total = jnp.zeros((16, D), F32)
    for c in range(8):
        total = total + dot_nt(children[c * 16 : (c + 1) * 16], maps[c])
    rest = jnp.concatenate([total[0:B3, 128:D], jnp.zeros((B3, 256 - D), F32)], axis=1)
    three = jnp.concatenate([total[0:B3, 0:128], rest], axis=0).astype(BF)
    send1[:, PACK:MESSAGE] = jnp.broadcast_to(three[None], (NCOL, 2 * B3, 128))
    ghost1[col] = send1[col]

    pl.semaphore_wait(barrier, NCOL - 1 + NROW - 1)

    def to_col1(i):
        peer = lax.rem(col + i, NCOL)
        return pltpu.make_async_remote_copy(
            src_ref=send1.at[peer], dst_ref=ghost1.at[col], send_sem=send_sem.at[0],
            recv_sem=recv_sem.at[0], device_id=(row, peer), device_id_type=MESH)

    def to_row2(i):
        peer = lax.rem(row + i, NROW)
        return pltpu.make_async_remote_copy(
            src_ref=send2.at[peer], dst_ref=ghost2.at[row], send_sem=send_sem.at[1],
            recv_sem=recv_sem.at[1], device_id=(peer, col), device_id_type=MESH)

    def start(copy):
        def step(i, _):
            copy(i).start()
            return 0
        return step

    lax.fori_loop(1, NCOL, start(to_col1), 0)
    lax.fori_loop(1, NROW, start(to_row2), 0)

    load_list.wait()

    def own(o, _):
        pick = hot(iota((B1, B1), 0) == list1_ref[pl.ds(o, 1), :])
        g[pl.ds(pl.multiple_of(o * D, D), D), 0:B1] = dot(one_ref[...], pick).astype(BF)
        return 0

    lax.fori_loop(0, NOFF, own, 0, unroll=8)

    load_trans.wait()
    for o in range(0, NOFF, 2):
        tcat[:, o * D : (o + 2) * D] = jnp.concatenate([trans[o], trans[o + 1]], axis=1)

    list2 = list2_ref[...]
    entries3 = as_row(list3_ref[...], B3)
    entries3 = entries3 + (entries3 & -8)
    pltpu.make_async_copy(ghost2.at[0 : NROW - 1], ghost2.at[0 : NROW - 1], recv_sem.at[1]).wait()
    tab2 = turned(jnp.concatenate([two, ghost2[...].reshape(NROW * GH2, D)], axis=0))
    g[:, B1:] = jnp.zeros((NOFF * D, 128), BF)
    for o in range(0, NOFF, 4):
        entries = jnp.concatenate([list2[o + j : o + j + 1, :] for j in range(4)], axis=1)
        pick = hot(iota((B2 + NROW * GH2, 4 * B2), 0) == entries)
        found = dot(tab2, pick).astype(BF)
        for j in range(4):
            g[(o + j) * D : (o + j + 1) * D, B1 : B1 + B2] = found[:, j * B2 : (j + 1) * B2]

    there = list1_ref[...] - B1
    there = jnp.where(
        there >= 0, ((there >> 4) & 1) * B1 + (there >> 5) * (GH1 // 2) + (there & 15), -1
    )
    list1_ref[...] = there
    pltpu.make_async_copy(ghost1.at[0 : NCOL - 1], ghost1.at[0 : NCOL - 1], recv_sem.at[0]).wait()
    half = GH1 // 2
    tab1[0:128, 0:B1] = turned(ghost1[:, 0:half].reshape(B1, 128))
    tab1[0:128, B1:] = turned(ghost1[:, half:GH1].reshape(B1, 128))
    rest = turned(ghost1[:, GH1:PACK].reshape(B1, 128))
    tab1[128:D, 0:B1] = rest[0 : D - 128]
    tab1[128:D, B1:] = rest[D - 128 :]

    tab3 = turned(ghost1[:, PACK:MESSAGE].reshape(NCOL * 16, 128))
    place = iota((NCOL * 16, NOFF * B3), 0)
    low = dot(tab3, hot(place == entries3))
    high = dot(tab3[0 : D - 128], hot(place == entries3 + 8))
    found = jnp.concatenate([low, high], axis=0).astype(BF)
    for o in range(NOFF):
        g[o * D : (o + 1) * D, B1 + B2 : B1 + B2 + B3] = found[:, o * B3 : (o + 1) * B3]

    def far(o, _):
        pick = hot(iota((NCOL * GH1, B1), 0) == list1_ref[pl.ds(o, 1), :])
        at = pl.ds(pl.multiple_of(o * D, D), D)
        g[at, 0:B1] = g[at, 0:B1] + dot(tab1[...], pick).astype(BF)
        return 0

    lax.fori_loop(0, NOFF, far, 0, unroll=8)
    total = dot(tcat[...], g[...])
    out1_ref[...] = total[:, 0:B1]
    both = total[:, B1:].T
    out2_ref[...] = 0.5 * both[0:B2]
    out3_ref[...] = 0.25 * both[B2 : B2 + B3]

    pltpu.make_async_copy(send1.at[0 : NCOL - 1], send1.at[0 : NCOL - 1], send_sem.at[0]).wait()
    pltpu.make_async_copy(send2.at[0 : NROW - 1], send2.at[0 : NROW - 1], send_sem.at[1]).wait()


def pass_on(*refs):
    for source, target in zip(refs[0:3], refs[3:6]):
        target[...] = source[...]


def on_device(
    level_one, child_maps, translations, send_one, list_one, send_two, list_two, list_three
):
    vmem = pl.BlockSpec(memory_space=pltpu.VMEM)
    any_ = pl.BlockSpec(memory_space=pl.ANY)
    shapes = (
        jax.ShapeDtypeStruct((D, B1), F32),
        jax.ShapeDtypeStruct((B2, D), F32),
        jax.ShapeDtypeStruct((B3, D), F32),
    )
    found = pl.pallas_call(
        kernel,
        out_shape=shapes,
        in_specs=[any_, vmem, any_, vmem, vmem, vmem, any_, any_],
        out_specs=(vmem, vmem, vmem),
        scratch_shapes=[
            pltpu.VMEM((D, B1), BF),
            pltpu.VMEM((NOFF, B1), jnp.int32),
            pltpu.VMEM((8, D, D), BF),
            pltpu.VMEM((NOFF, D, D), BF),
            pltpu.VMEM((D, NOFF * D), BF),
            pltpu.VMEM((NCOL, MESSAGE, 128), BF),
            pltpu.VMEM((NCOL, MESSAGE, 128), BF),
            pltpu.VMEM((NROW, GH2, D), BF),
            pltpu.VMEM((NROW, GH2, D), BF),
            pltpu.VMEM((NOFF * D, B1 + 128), BF),
            pltpu.VMEM((D, NCOL * GH1), BF),
            pltpu.SemaphoreType.DMA((4,)),
            pltpu.SemaphoreType.DMA((2,)),
            pltpu.SemaphoreType.DMA((2,)),
        ],
        compiler_params=pltpu.CompilerParams(
            collective_id=0, has_side_effects=True, vmem_limit_bytes=60 << 20
        ),
    )(
        level_one, send_one.reshape(NCOL, GH1), list_one.T, send_two.reshape(NROW, GH2),
        list_two.T, list_three, child_maps, translations,
    )
    out1, out2, out3 = pl.pallas_call(
        pass_on,
        out_shape=shapes,
        in_specs=[vmem] * 3,
        out_specs=(vmem,) * 3,
    )(*found)
    return out1, out2.T, out3.T


def solution(mesh):
    placed = (
        P(None, ("row", "col")),
        P(),
        P(),
        P(("row", "col"), None, None),
        P(("row", "col"), None),
        P(("row", "col"), None, None),
        P(("row", "col"), None),
        P(("row", "col"), None),
    )
    return jax.shard_map(
        on_device,
        mesh=mesh,
        in_specs=placed,
        out_specs=(P(None, ("row", "col")), P(None, ("row", "col")), P(None, ("row", "col"))),
        check_vma=False,
    )
```

```python
import jax
import jax.numpy as jnp
from jax import lax
from jax.experimental import pallas as pl
from jax.experimental.pallas import tpu as pltpu
from jax.sharding import PartitionSpec as P

BF = jnp.bfloat16
F32 = jnp.float32
NT = (((1,), (1,)), ((), ()))
D, NOFF, B1, B2, B3 = 192, 32, 512, 64, 8
NCOL, NROW, GH1, GH2 = 32, 16, 32, 16
GROUP = 8
CHUNK = 8
PACK = 48
MESSAGE = PACK + 2 * B3
MESH = pl.DeviceIdType.MESH


def iota(shape, axis):
    return lax.broadcasted_iota(jnp.int32, shape, axis)


def dot(a, b):
    return jnp.dot(a, b, preferred_element_type=F32)


def dot_nt(a, b):
    return lax.dot_general(a, b, NT, preferred_element_type=F32)


def hot(mask):
    return jnp.where(mask, 1.0, 0.0).astype(BF)


def turned(table):
    w = table.shape[1]
    eye = hot(iota((w, w), 0) == iota((w, w), 1))
    return dot_nt(eye, table).astype(BF)


def as_row(entries, width):
    k, p = entries.shape
    n = p * width
    spread = hot(iota((p, n), 1) // width == iota((p, n), 0))
    wide = dot(entries.astype(F32).astype(BF), spread)
    keep = iota((k, n), 1) % width == iota((k, n), 0)
    return jnp.sum(jnp.where(keep, wide, 0.0), axis=0, keepdims=True).astype(jnp.int32)


def kernel(
    one_hbm, send1_ref, list1_hbm, send2_ref, list2_ref, list3_ref, maps_hbm, trans_hbm,
    out1_ref, out2_ref, out3_ref,
    one_ref, list1_ref, maps, trans, tcat, send1, ghost1, send2, ghost2, g, tab1,
    load_sem, send_sem, recv_sem, plane_sem, all_sem,
):
    row = lax.axis_index("row")
    col = lax.axis_index("col")
    barrier = pltpu.get_barrier_semaphore()

    gate = lax.rem(col, GROUP) == 0

    def hello(i, _):
        peer = lax.rem(col + i, NCOL)

        @pl.when(lax.rem(peer, GROUP) != 0)
        def _():
            pl.semaphore_signal(barrier, inc=1, device_id=(row, peer), device_id_type=MESH)

        return 0

    load_one = pltpu.make_async_copy(one_hbm, one_ref, load_sem.at[0])
    load_one.start()
    load_maps = pltpu.make_async_copy(maps_hbm, maps, load_sem.at[1])
    load_maps.start()
    lax.fori_loop(1, NCOL, hello, 0)
    load_list = pltpu.make_async_copy(list1_hbm, list1_ref, load_sem.at[2])
    load_trans = pltpu.make_async_copy(trans_hbm, trans, load_sem.at[3])
    load_list.start()
    load_trans.start()

    who = send1_ref[...].T
    lane = iota((GH1, B1), 1)
    load_one.wait()
    for p0 in range(0, NCOL, 8):
        pick = jnp.concatenate([hot(who[:, p : p + 1] == lane) for p in range(p0, p0 + 8)], axis=0)
        rows = dot_nt(pick, one_ref[...]).reshape(8, GH1, D)
        send1[p0 : p0 + 8, 0:GH1] = rows[:, :, 0:128].astype(BF)
        rest = rows[:, :, 128:D]
        rest = jnp.concatenate([rest[:, 0 : GH1 // 2], rest[:, GH1 // 2 :]], axis=2)
        send1[p0 : p0 + 8, GH1:PACK] = rest.astype(BF)
    load_maps.wait()
    r = iota((B1, B1), 0)
    pick = hot(iota((B1, B1), 1) == (r & (B2 - 1)) * 8 + (r >> 6))
    children = dot_nt(pick, one_ref[...]).astype(BF)
    total = jnp.zeros((B2, D), F32)
    for c in range(8):
        total = total + dot_nt(children[c * B2 : (c + 1) * B2], maps[c])
    two = total.astype(BF)
    who = send2_ref[...].T
    lane = iota((GH2, B2), 1)
    pick = jnp.concatenate([hot(who[:, p : p + 1] == lane) for p in range(NROW)], axis=0)
    send2[...] = dot(pick, two).astype(BF).reshape(NROW, GH2, D)
    ghost2[row] = send2[row]

    r = iota((128, B2), 0)
    pick = hot(iota((128, B2), 1) == (r & 15) * 8 + (r >> 4))
    children = dot(pick, two).astype(BF)
    total = jnp.zeros((16, D), F32)
    for c in range(8):
        total = total + dot_nt(children[c * 16 : (c + 1) * 16], maps[c])
    rest = jnp.concatenate([total[0:B3, 128:D], jnp.zeros((B3, 256 - D), F32)], axis=1)
    three = jnp.concatenate([total[0:B3, 0:128], rest], axis=0).astype(BF)
    send1[:, PACK:MESSAGE] = jnp.broadcast_to(three[None], (NCOL, 2 * B3, 128))
    ghost1[col] = send1[col]

    @pl.when(jnp.logical_not(gate))
    def _():
        pl.semaphore_wait(barrier, NCOL - 1)

        def tell(q, _):
            pl.semaphore_signal(plane_sem, inc=1, device_id=(row, q * GROUP), device_id_type=MESH)
            return 0

        lax.fori_loop(0, NCOL // GROUP, tell, 0)

    @pl.when(gate)
    def _():
        pl.semaphore_wait(plane_sem, NCOL - NCOL // GROUP)

        def tell(i, _):
            pl.semaphore_signal(
                barrier, inc=1, device_id=(lax.rem(row + i, NROW), col), device_id_type=MESH
            )
            return 0

        lax.fori_loop(1, NROW, tell, 0)

    def to_col1(i):
        peer = lax.rem(col + i, NCOL)
        return pltpu.make_async_remote_copy(
            src_ref=send1.at[peer], dst_ref=ghost1.at[col], send_sem=send_sem.at[0],
            recv_sem=recv_sem.at[0], device_id=(row, peer), device_id_type=MESH)

    def to_row2(i):
        peer = lax.rem(row + i, NROW)
        return pltpu.make_async_remote_copy(
            src_ref=send2.at[peer], dst_ref=ghost2.at[row], send_sem=send_sem.at[1],
            recv_sem=recv_sem.at[1], device_id=(peer, col), device_id_type=MESH)

    def start(copy):
        def step(i, _):
            copy(i).start()
            return 0
        return step

    lax.fori_loop(1, NCOL, start(to_col1), 0)

    load_list.wait()

    def own(o, _):
        pick = hot(iota((B1, B1), 0) == list1_ref[pl.ds(o, 1), :])
        g[pl.ds(pl.multiple_of(o * D, D), D), 0:B1] = dot(one_ref[...], pick).astype(BF)
        return 0

    lax.fori_loop(0, NOFF, own, 0, unroll=8)

    load_trans.wait()
    for o in range(0, NOFF, 2):
        tcat[:, o * D : (o + 2) * D] = jnp.concatenate([trans[o], trans[o + 1]], axis=1)

    list2 = list2_ref[...]
    entries3 = as_row(list3_ref[...], B3)
    entries3 = entries3 + (entries3 & -8)
    g[:, B1:] = jnp.zeros((NOFF * D, 128), BF)

    there = list1_ref[...] - B1
    there = jnp.where(
        there >= 0, ((there >> 4) & 1) * B1 + (there >> 5) * (GH1 // 2) + (there & 15), -1
    )
    list1_ref[...] = there
    pltpu.make_async_copy(ghost1.at[0 : NCOL - 1], ghost1.at[0 : NCOL - 1], recv_sem.at[0]).wait()
    half = GH1 // 2
    tab1[0:128, 0:B1] = turned(ghost1[:, 0:half].reshape(B1, 128))
    tab1[0:128, B1:] = turned(ghost1[:, half:GH1].reshape(B1, 128))
    rest = turned(ghost1[:, GH1:PACK].reshape(B1, 128))
    tab1[128:D, 0:B1] = rest[0 : D - 128]
    tab1[128:D, B1:] = rest[D - 128 :]

    tab3 = turned(ghost1[:, PACK:MESSAGE].reshape(NCOL * 16, 128))
    place = iota((NCOL * 16, NOFF * B3), 0)
    low = dot(tab3, hot(place == entries3))
    high = dot(tab3[0 : D - 128], hot(place == entries3 + 8))
    found = jnp.concatenate([low, high], axis=0).astype(BF)
    for o in range(NOFF):
        g[o * D : (o + 1) * D, B1 + B2 : B1 + B2 + B3] = found[:, o * B3 : (o + 1) * B3]

    def far(o, _):
        pick = hot(iota((NCOL * GH1, B1), 0) == list1_ref[pl.ds(o, 1), :])
        at = pl.ds(pl.multiple_of(o * D, D), D)
        g[at, 0:B1] = g[at, 0:B1] + dot(tab1[...], pick).astype(BF)
        return 0

    def across():
        @pl.when(gate)
        def _():
            pl.semaphore_wait(barrier, NROW - 1)

            def tell(i, _):
                pl.semaphore_signal(all_sem, inc=1, device_id=(row, col + i), device_id_type=MESH)
                return 0

            lax.fori_loop(1, GROUP, tell, 0)

        @pl.when(jnp.logical_not(gate))
        def _():
            pl.semaphore_wait(all_sem, 1)

        lax.fori_loop(1, NROW, start(to_row2), 0)

    place = jnp.maximum(2 - row // 4, 0)

    def chunk(n, _):
        pl.when(n == place)(across)

        def step(k, _):
            return far(n * CHUNK + k, 0)

        return lax.fori_loop(0, CHUNK, step, 0, unroll=True)

    lax.fori_loop(0, NOFF // CHUNK, chunk, 0)
    out1_ref[...] = dot(tcat[...], g[:, 0:B1])

    pltpu.make_async_copy(ghost2.at[0 : NROW - 1], ghost2.at[0 : NROW - 1], recv_sem.at[1]).wait()
    tab2 = turned(jnp.concatenate([two, ghost2[...].reshape(NROW * GH2, D)], axis=0))
    for o in range(0, NOFF, 4):
        entries = jnp.concatenate([list2[o + j : o + j + 1, :] for j in range(4)], axis=1)
        pick = hot(iota((B2 + NROW * GH2, 4 * B2), 0) == entries)
        found = dot(tab2, pick).astype(BF)
        for j in range(4):
            g[(o + j) * D : (o + j + 1) * D, B1 : B1 + B2] = found[:, j * B2 : (j + 1) * B2]

    both = dot(tcat[...], g[:, B1:]).T
    out2_ref[...] = 0.5 * both[0:B2]
    out3_ref[...] = 0.25 * both[B2 : B2 + B3]

    pltpu.make_async_copy(send1.at[0 : NCOL - 1], send1.at[0 : NCOL - 1], send_sem.at[0]).wait()
    pltpu.make_async_copy(send2.at[0 : NROW - 1], send2.at[0 : NROW - 1], send_sem.at[1]).wait()


def pass_on(*refs):
    for source, target in zip(refs[0:3], refs[3:6]):
        target[...] = source[...]


def on_device(
    level_one, child_maps, translations, send_one, list_one, send_two, list_two, list_three
):
    vmem = pl.BlockSpec(memory_space=pltpu.VMEM)
    any_ = pl.BlockSpec(memory_space=pl.ANY)
    shapes = (
        jax.ShapeDtypeStruct((D, B1), F32),
        jax.ShapeDtypeStruct((B2, D), F32),
        jax.ShapeDtypeStruct((B3, D), F32),
    )
    found = pl.pallas_call(
        kernel,
        out_shape=shapes,
        in_specs=[any_, vmem, any_, vmem, vmem, vmem, any_, any_],
        out_specs=(vmem, vmem, vmem),
        scratch_shapes=[
            pltpu.VMEM((D, B1), BF),
            pltpu.VMEM((NOFF, B1), jnp.int32),
            pltpu.VMEM((8, D, D), BF),
            pltpu.VMEM((NOFF, D, D), BF),
            pltpu.VMEM((D, NOFF * D), BF),
            pltpu.VMEM((NCOL, MESSAGE, 128), BF),
            pltpu.VMEM((NCOL, MESSAGE, 128), BF),
            pltpu.VMEM((NROW, GH2, D), BF),
            pltpu.VMEM((NROW, GH2, D), BF),
            pltpu.VMEM((NOFF * D, B1 + 128), BF),
            pltpu.VMEM((D, NCOL * GH1), BF),
            pltpu.SemaphoreType.DMA((4,)),
            pltpu.SemaphoreType.DMA((2,)),
            pltpu.SemaphoreType.DMA((2,)),
            pltpu.SemaphoreType.REGULAR,
            pltpu.SemaphoreType.REGULAR,
        ],
        compiler_params=pltpu.CompilerParams(
            collective_id=0, has_side_effects=True, vmem_limit_bytes=60 << 20
        ),
    )(
        level_one, send_one.reshape(NCOL, GH1), list_one.T, send_two.reshape(NROW, GH2),
        list_two.T, list_three, child_maps, translations,
    )
    out1, out2, out3 = pl.pallas_call(
        pass_on,
        out_shape=shapes,
        in_specs=[vmem] * 3,
        out_specs=(vmem,) * 3,
    )(*found)
    return out1, out2.T, out3.T


def solution(mesh):
    placed = (
        P(None, ("row", "col")),
        P(),
        P(),
        P(("row", "col"), None, None),
        P(("row", "col"), None),
        P(("row", "col"), None, None),
        P(("row", "col"), None),
        P(("row", "col"), None),
    )
    return jax.shard_map(
        on_device,
        mesh=mesh,
        in_specs=placed,
        out_specs=(P(None, ("row", "col")), P(None, ("row", "col")), P(None, ("row", "col"))),
        check_vma=False,
    )
```

```python
import jax
import jax.numpy as jnp
from jax import lax
from jax.experimental import pallas as pl
from jax.experimental.pallas import tpu as pltpu
from jax.sharding import PartitionSpec as P

BF = jnp.bfloat16
F32 = jnp.float32
NT = (((1,), (1,)), ((), ()))
D, NOFF, B1, B2, B3 = 192, 32, 512, 64, 8
NCOL, NROW, GH1, GH2 = 32, 16, 32, 16
GROUP = 8
CHUNK = 8
SLOTS = NOFF // CHUNK
PACK = 48
MESSAGE = PACK + 2 * B3
MESH = pl.DeviceIdType.MESH


def iota(shape, axis):
    return lax.broadcasted_iota(jnp.int32, shape, axis)


def dot(a, b):
    return jnp.dot(a, b, preferred_element_type=F32)


def dot_nt(a, b):
    return lax.dot_general(a, b, NT, preferred_element_type=F32)


def hot(mask):
    return jnp.where(mask, 1.0, 0.0).astype(BF)


def turned(table):
    w = table.shape[1]
    eye = hot(iota((w, w), 0) == iota((w, w), 1))
    return dot_nt(eye, table).astype(BF)


def as_row(entries, width):
    k, p = entries.shape
    n = p * width
    spread = hot(iota((p, n), 1) // width == iota((p, n), 0))
    wide = dot(entries.astype(F32).astype(BF), spread)
    keep = iota((k, n), 1) % width == iota((k, n), 0)
    return jnp.sum(jnp.where(keep, wide, 0.0), axis=0, keepdims=True).astype(jnp.int32)


def kernel(
    one_hbm, send1_ref, list1_hbm, send2_ref, list2_ref, list3_ref, maps_hbm, trans_hbm,
    out1_ref, out2_ref, out3_ref,
    one_ref, list1_ref, maps, trans, tcat, send1, ghost1, send2, ghost2, g, tab1,
    load_sem, send_sem, recv_sem, plane_sem, all_sem,
):
    row = lax.axis_index("row")
    col = lax.axis_index("col")
    barrier = pltpu.get_barrier_semaphore()

    gate = lax.rem(col, GROUP) == 0

    def hello(i, _):
        peer = lax.rem(col + i, NCOL)

        @pl.when(lax.rem(peer, GROUP) != 0)
        def _():
            pl.semaphore_signal(barrier, inc=1, device_id=(row, peer), device_id_type=MESH)

        return 0

    load_one = pltpu.make_async_copy(one_hbm, one_ref, load_sem.at[0])
    load_one.start()
    load_maps = pltpu.make_async_copy(maps_hbm, maps, load_sem.at[1])
    load_maps.start()
    lax.fori_loop(1, NCOL, hello, 0)
    load_list = pltpu.make_async_copy(list1_hbm, list1_ref, load_sem.at[2])
    load_trans = pltpu.make_async_copy(trans_hbm, trans, load_sem.at[3])
    load_list.start()
    load_trans.start()

    who = send1_ref[...].T
    lane = iota((GH1, B1), 1)
    load_one.wait()
    for p0 in range(0, NCOL, 8):
        pick = jnp.concatenate([hot(who[:, p : p + 1] == lane) for p in range(p0, p0 + 8)], axis=0)
        rows = dot_nt(pick, one_ref[...]).reshape(8, GH1, D)
        send1[p0 : p0 + 8, 0:GH1] = rows[:, :, 0:128].astype(BF)
        rest = rows[:, :, 128:D]
        rest = jnp.concatenate([rest[:, 0 : GH1 // 2], rest[:, GH1 // 2 :]], axis=2)
        send1[p0 : p0 + 8, GH1:PACK] = rest.astype(BF)

    @pl.when(jnp.logical_not(gate))
    def _():
        pl.semaphore_wait(barrier, NCOL - 1)

        def tell(q, _):
            pl.semaphore_signal(plane_sem, inc=1, device_id=(row, q * GROUP), device_id_type=MESH)
            return 0

        lax.fori_loop(0, NCOL // GROUP, tell, 0)

    load_maps.wait()
    r = iota((B1, B1), 0)
    pick = hot(iota((B1, B1), 1) == (r & (B2 - 1)) * 8 + (r >> 6))
    children = dot_nt(pick, one_ref[...]).astype(BF)
    total = jnp.zeros((B2, D), F32)
    for c in range(8):
        total = total + dot_nt(children[c * B2 : (c + 1) * B2], maps[c])
    two = total.astype(BF)
    who = send2_ref[...].T
    lane = iota((GH2, B2), 1)
    pick = jnp.concatenate([hot(who[:, p : p + 1] == lane) for p in range(NROW)], axis=0)
    send2[...] = dot(pick, two).astype(BF).reshape(NROW, GH2, D)
    ghost2[row] = send2[row]

    r = iota((128, B2), 0)
    pick = hot(iota((128, B2), 1) == (r & 15) * 8 + (r >> 4))
    children = dot(pick, two).astype(BF)
    total = jnp.zeros((16, D), F32)
    for c in range(8):
        total = total + dot_nt(children[c * 16 : (c + 1) * 16], maps[c])
    rest = jnp.concatenate([total[0:B3, 128:D], jnp.zeros((B3, 256 - D), F32)], axis=1)
    three = jnp.concatenate([total[0:B3, 0:128], rest], axis=0).astype(BF)
    send1[:, PACK:MESSAGE] = jnp.broadcast_to(three[None], (NCOL, 2 * B3, 128))
    ghost1[col] = send1[col]

    @pl.when(gate)
    def _():
        pl.semaphore_wait(plane_sem, NCOL - NCOL // GROUP)

        def tell(i, _):
            pl.semaphore_signal(
                barrier, inc=1, device_id=(lax.rem(row + i, NROW), col), device_id_type=MESH
            )
            return 0

        lax.fori_loop(1, NROW, tell, 0)

    def to_col1(i):
        peer = lax.rem(col + i, NCOL)
        return pltpu.make_async_remote_copy(
            src_ref=send1.at[peer], dst_ref=ghost1.at[col], send_sem=send_sem.at[0],
            recv_sem=recv_sem.at[0], device_id=(row, peer), device_id_type=MESH)

    def to_row2(i):
        peer = lax.rem(row + i, NROW)
        return pltpu.make_async_remote_copy(
            src_ref=send2.at[peer], dst_ref=ghost2.at[row], send_sem=send_sem.at[1],
            recv_sem=recv_sem.at[1], device_id=(peer, col), device_id_type=MESH)

    def start(copy):
        def step(i, _):
            copy(i).start()
            return 0
        return step

    lax.fori_loop(1, NCOL, start(to_col1), 0)

    def across():
        @pl.when(gate)
        def _():
            pl.semaphore_wait(barrier, NROW - 1)

            def tell(i, _):
                pl.semaphore_signal(all_sem, inc=1, device_id=(row, col + i), device_id_type=MESH)
                return 0

            lax.fori_loop(1, GROUP, tell, 0)

        @pl.when(jnp.logical_not(gate))
        def _():
            pl.semaphore_wait(all_sem, 1)

        lax.fori_loop(1, NROW, start(to_row2), 0)

    turn = jnp.where(row < 4, 5, 3)

    def chunks(work, before):
        def chunk(n, _):
            pl.when(n + before == turn)(across)

            def step(k, _):
                return work(n * CHUNK + k, 0)

            return lax.fori_loop(0, CHUNK, step, 0, unroll=True)

        return chunk

    load_list.wait()

    def own(o, _):
        pick = hot(iota((B1, B1), 0) == list1_ref[pl.ds(o, 1), :])
        g[pl.ds(pl.multiple_of(o * D, D), D), 0:B1] = dot(one_ref[...], pick).astype(BF)
        return 0

    lax.fori_loop(0, SLOTS, chunks(own, 0), 0)

    load_trans.wait()
    for o in range(0, NOFF, 2):
        tcat[:, o * D : (o + 2) * D] = jnp.concatenate([trans[o], trans[o + 1]], axis=1)

    list2 = list2_ref[...]
    entries3 = as_row(list3_ref[...], B3)
    entries3 = entries3 + (entries3 & -8)
    g[:, B1:] = jnp.zeros((NOFF * D, 128), BF)

    there = list1_ref[...] - B1
    there = jnp.where(
        there >= 0, ((there >> 4) & 1) * B1 + (there >> 5) * (GH1 // 2) + (there & 15), -1
    )
    list1_ref[...] = there
    pltpu.make_async_copy(ghost1.at[0 : NCOL - 1], ghost1.at[0 : NCOL - 1], recv_sem.at[0]).wait()
    half = GH1 // 2
    tab1[0:128, 0:B1] = turned(ghost1[:, 0:half].reshape(B1, 128))
    tab1[0:128, B1:] = turned(ghost1[:, half:GH1].reshape(B1, 128))
    rest = turned(ghost1[:, GH1:PACK].reshape(B1, 128))
    tab1[128:D, 0:B1] = rest[0 : D - 128]
    tab1[128:D, B1:] = rest[D - 128 :]

    tab3 = turned(ghost1[:, PACK:MESSAGE].reshape(NCOL * 16, 128))
    place = iota((NCOL * 16, NOFF * B3), 0)
    low = dot(tab3, hot(place == entries3))
    high = dot(tab3[0 : D - 128], hot(place == entries3 + 8))
    found = jnp.concatenate([low, high], axis=0).astype(BF)
    for o in range(NOFF):
        g[o * D : (o + 1) * D, B1 + B2 : B1 + B2 + B3] = found[:, o * B3 : (o + 1) * B3]

    def far(o, _):
        pick = hot(iota((NCOL * GH1, B1), 0) == list1_ref[pl.ds(o, 1), :])
        at = pl.ds(pl.multiple_of(o * D, D), D)
        g[at, 0:B1] = g[at, 0:B1] + dot(tab1[...], pick).astype(BF)
        return 0

    lax.fori_loop(0, SLOTS, chunks(far, SLOTS), 0)
    out1_ref[...] = dot(tcat[...], g[:, 0:B1])

    pltpu.make_async_copy(ghost2.at[0 : NROW - 1], ghost2.at[0 : NROW - 1], recv_sem.at[1]).wait()
    tab2 = turned(jnp.concatenate([two, ghost2[...].reshape(NROW * GH2, D)], axis=0))
    for o in range(0, NOFF, 4):
        entries = jnp.concatenate([list2[o + j : o + j + 1, :] for j in range(4)], axis=1)
        pick = hot(iota((B2 + NROW * GH2, 4 * B2), 0) == entries)
        found = dot(tab2, pick).astype(BF)
        for j in range(4):
            g[(o + j) * D : (o + j + 1) * D, B1 : B1 + B2] = found[:, j * B2 : (j + 1) * B2]

    both = dot(tcat[...], g[:, B1:]).T
    out2_ref[...] = 0.5 * both[0:B2]
    out3_ref[...] = 0.25 * both[B2 : B2 + B3]

    pltpu.make_async_copy(send1.at[0 : NCOL - 1], send1.at[0 : NCOL - 1], send_sem.at[0]).wait()
    pltpu.make_async_copy(send2.at[0 : NROW - 1], send2.at[0 : NROW - 1], send_sem.at[1]).wait()


def pass_on(*refs):
    for source, target in zip(refs[0:3], refs[3:6]):
        target[...] = source[...]


def on_device(
    level_one, child_maps, translations, send_one, list_one, send_two, list_two, list_three
):
    vmem = pl.BlockSpec(memory_space=pltpu.VMEM)
    any_ = pl.BlockSpec(memory_space=pl.ANY)
    shapes = (
        jax.ShapeDtypeStruct((D, B1), F32),
        jax.ShapeDtypeStruct((B2, D), F32),
        jax.ShapeDtypeStruct((B3, D), F32),
    )
    found = pl.pallas_call(
        kernel,
        out_shape=shapes,
        in_specs=[any_, vmem, any_, vmem, vmem, vmem, any_, any_],
        out_specs=(vmem, vmem, vmem),
        scratch_shapes=[
            pltpu.VMEM((D, B1), BF),
            pltpu.VMEM((NOFF, B1), jnp.int32),
            pltpu.VMEM((8, D, D), BF),
            pltpu.VMEM((NOFF, D, D), BF),
            pltpu.VMEM((D, NOFF * D), BF),
            pltpu.VMEM((NCOL, MESSAGE, 128), BF),
            pltpu.VMEM((NCOL, MESSAGE, 128), BF),
            pltpu.VMEM((NROW, GH2, D), BF),
            pltpu.VMEM((NROW, GH2, D), BF),
            pltpu.VMEM((NOFF * D, B1 + 128), BF),
            pltpu.VMEM((D, NCOL * GH1), BF),
            pltpu.SemaphoreType.DMA((4,)),
            pltpu.SemaphoreType.DMA((2,)),
            pltpu.SemaphoreType.DMA((2,)),
            pltpu.SemaphoreType.REGULAR,
            pltpu.SemaphoreType.REGULAR,
        ],
        compiler_params=pltpu.CompilerParams(
            collective_id=0, has_side_effects=True, vmem_limit_bytes=60 << 20
        ),
    )(
        level_one, send_one.reshape(NCOL, GH1), list_one.T, send_two.reshape(NROW, GH2),
        list_two.T, list_three, child_maps, translations,
    )
    out1, out2, out3 = pl.pallas_call(
        pass_on,
        out_shape=shapes,
        in_specs=[vmem] * 3,
        out_specs=(vmem,) * 3,
    )(*found)
    return out1, out2.T, out3.T


def solution(mesh):
    placed = (
        P(None, ("row", "col")),
        P(),
        P(),
        P(("row", "col"), None, None),
        P(("row", "col"), None),
        P(("row", "col"), None, None),
        P(("row", "col"), None),
        P(("row", "col"), None),
    )
    return jax.shard_map(
        on_device,
        mesh=mesh,
        in_specs=placed,
        out_specs=(P(None, ("row", "col")), P(None, ("row", "col")), P(None, ("row", "col"))),
        check_vma=False,
    )
```

```python
import jax
import jax.numpy as jnp
from jax import lax
from jax.experimental import pallas as pl
from jax.experimental.pallas import tpu as pltpu
from jax.sharding import PartitionSpec as P

BF = jnp.bfloat16
F32 = jnp.float32
NT = (((1,), (1,)), ((), ()))
D, NOFF, B1, B2, B3 = 192, 32, 512, 64, 8
NCOL, NROW, GH1, GH2 = 32, 16, 32, 16
GROUP = 8
CHUNK = 8
SLOTS = NOFF // CHUNK
PACK = 48
MESSAGE = PACK + 2 * B3
MESH = pl.DeviceIdType.MESH


def iota(shape, axis):
    return lax.broadcasted_iota(jnp.int32, shape, axis)


def dot(a, b):
    return jnp.dot(a, b, preferred_element_type=F32)


def dot_nt(a, b):
    return lax.dot_general(a, b, NT, preferred_element_type=F32)


def hot(mask):
    return jnp.where(mask, 1.0, 0.0).astype(BF)


def turned(table):
    w = table.shape[1]
    eye = hot(iota((w, w), 0) == iota((w, w), 1))
    return dot_nt(eye, table).astype(BF)


def as_row(entries, width):
    k, p = entries.shape
    n = p * width
    spread = hot(iota((p, n), 1) // width == iota((p, n), 0))
    wide = dot(entries.astype(F32).astype(BF), spread)
    keep = iota((k, n), 1) % width == iota((k, n), 0)
    return jnp.sum(jnp.where(keep, wide, 0.0), axis=0, keepdims=True).astype(jnp.int32)


def kernel(
    one_hbm, send1_hbm, list1_hbm, send2_hbm, list2_hbm, list3_hbm, maps_hbm, trans_hbm,
    out1_ref, out2_ref, out3_ref,
    one_ref, list1_ref, maps, trans, tcat, send1, ghost1, send2, ghost2, g, tab1,
    send1_ref, send2_ref, list2_ref, list3_ref, far1, load_sem, send_sem, recv_sem, plane_sem, all_sem,
):
    row = lax.axis_index("row")
    col = lax.axis_index("col")
    barrier = pltpu.get_barrier_semaphore()

    gate = lax.rem(col, GROUP) == 0

    def hello(i, _):
        peer = lax.rem(col + i, NCOL)

        @pl.when(lax.rem(peer, GROUP) != 0)
        def _():
            pl.semaphore_signal(barrier, inc=1, device_id=(row, peer), device_id_type=MESH)

        return 0

    load_one = pltpu.make_async_copy(one_hbm, one_ref, load_sem.at[0])
    load_one.start()
    load_send1 = pltpu.make_async_copy(send1_hbm, send1_ref, load_sem.at[4])
    load_send2 = pltpu.make_async_copy(send2_hbm, send2_ref, load_sem.at[5])
    load_list2 = pltpu.make_async_copy(list2_hbm, list2_ref, load_sem.at[6])
    load_list3 = pltpu.make_async_copy(list3_hbm, list3_ref, load_sem.at[7])
    load_send1.start()
    load_send2.start()
    load_list2.start()
    load_list3.start()
    load_maps = pltpu.make_async_copy(maps_hbm, maps, load_sem.at[1])
    load_maps.start()
    lax.fori_loop(1, NCOL, hello, 0)
    load_list = pltpu.make_async_copy(list1_hbm, list1_ref, load_sem.at[2])
    load_trans = pltpu.make_async_copy(trans_hbm, trans, load_sem.at[3])
    load_list.start()
    load_trans.start()

    load_send1.wait()
    who = send1_ref[...].T
    lane = iota((GH1, B1), 1)
    load_one.wait()
    for p0 in range(0, NCOL, 8):
        pick = jnp.concatenate([hot(who[:, p : p + 1] == lane) for p in range(p0, p0 + 8)], axis=0)
        rows = dot_nt(pick, one_ref[...]).reshape(8, GH1, D)
        send1[p0 : p0 + 8, 0:GH1] = rows[:, :, 0:128].astype(BF)
        rest = rows[:, :, 128:D]
        rest = jnp.concatenate([rest[:, 0 : GH1 // 2], rest[:, GH1 // 2 :]], axis=2)
        send1[p0 : p0 + 8, GH1:PACK] = rest.astype(BF)

    @pl.when(jnp.logical_not(gate))
    def _():
        pl.semaphore_wait(barrier, NCOL - 1)

        def tell(q, _):
            pl.semaphore_signal(plane_sem, inc=1, device_id=(row, q * GROUP), device_id_type=MESH)
            return 0

        lax.fori_loop(0, NCOL // GROUP, tell, 0)

    load_maps.wait()
    r = iota((B1, B1), 0)
    pick = hot(iota((B1, B1), 1) == (r & (B2 - 1)) * 8 + (r >> 6))
    children = dot_nt(pick, one_ref[...]).astype(BF)
    total = jnp.zeros((B2, D), F32)
    for c in range(8):
        total = total + dot_nt(children[c * B2 : (c + 1) * B2], maps[c])
    two = total.astype(BF)
    load_send2.wait()
    who = send2_ref[...].T
    lane = iota((GH2, B2), 1)
    pick = jnp.concatenate([hot(who[:, p : p + 1] == lane) for p in range(NROW)], axis=0)
    send2[...] = dot(pick, two).astype(BF).reshape(NROW, GH2, D)
    ghost2[row] = send2[row]

    r = iota((128, B2), 0)
    pick = hot(iota((128, B2), 1) == (r & 15) * 8 + (r >> 4))
    children = dot(pick, two).astype(BF)
    total = jnp.zeros((16, D), F32)
    for c in range(8):
        total = total + dot_nt(children[c * 16 : (c + 1) * 16], maps[c])
    rest = jnp.concatenate([total[0:B3, 128:D], jnp.zeros((B3, 256 - D), F32)], axis=1)
    three = jnp.concatenate([total[0:B3, 0:128], rest], axis=0).astype(BF)
    send1[:, PACK:MESSAGE] = jnp.broadcast_to(three[None], (NCOL, 2 * B3, 128))
    ghost1[col] = send1[col]

    @pl.when(gate)
    def _():
        pl.semaphore_wait(plane_sem, NCOL - NCOL // GROUP)

        def tell(i, _):
            pl.semaphore_signal(
                barrier, inc=1, device_id=(lax.rem(row + i, NROW), col), device_id_type=MESH
            )
            return 0

        lax.fori_loop(1, NROW, tell, 0)

    def to_col1(i):
        peer = lax.rem(col + i, NCOL)
        return pltpu.make_async_remote_copy(
            src_ref=send1.at[peer], dst_ref=ghost1.at[col], send_sem=send_sem.at[0],
            recv_sem=recv_sem.at[0], device_id=(row, peer), device_id_type=MESH)

    def to_row2(i):
        peer = lax.rem(row + i, NROW)
        return pltpu.make_async_remote_copy(
            src_ref=send2.at[peer], dst_ref=ghost2.at[row], send_sem=send_sem.at[1],
            recv_sem=recv_sem.at[1], device_id=(peer, col), device_id_type=MESH)

    def start(copy):
        def step(i, _):
            copy(i).start()
            return 0
        return step

    lax.fori_loop(1, NCOL, start(to_col1), 0)

    def across():
        @pl.when(gate)
        def _():
            pl.semaphore_wait(barrier, NROW - 1)

            def tell(i, _):
                pl.semaphore_signal(all_sem, inc=1, device_id=(row, col + i), device_id_type=MESH)
                return 0

            lax.fori_loop(1, GROUP, tell, 0)

        @pl.when(jnp.logical_not(gate))
        def _():
            pl.semaphore_wait(all_sem, 1)

        lax.fori_loop(1, NROW, start(to_row2), 0)

    turn = jnp.where(row < 4, 5, 3)

    def chunks(work, before):
        def chunk(n, _):
            pl.when(n + before == turn)(across)

            def step(k, _):
                return work(n * CHUNK + k, 0)

            return lax.fori_loop(0, CHUNK, step, 0, unroll=True)

        return chunk

    load_list.wait()

    def own(o, _):
        pick = hot(iota((B1, B1), 0) == list1_ref[pl.ds(o, 1), :])
        g[pl.ds(pl.multiple_of(o * D, D), D), 0:B1] = dot(one_ref[...], pick).astype(BF)
        return 0

    lax.fori_loop(0, SLOTS, chunks(own, 0), 0)

    load_trans.wait()
    for o in range(0, NOFF, 2):
        tcat[:, o * D : (o + 2) * D] = jnp.concatenate([trans[o], trans[o + 1]], axis=1)

    load_list2.wait()
    load_list3.wait()
    list2 = list2_ref[...]
    entries3 = as_row(list3_ref[...], B3)
    entries3 = entries3 + (entries3 & -8)
    g[:, B1:] = jnp.zeros((NOFF * D, 128), BF)

    there = list1_ref[...] - B1
    there = jnp.where(
        there >= 0, ((there >> 4) & 1) * B1 + (there >> 5) * (GH1 // 2) + (there & 15), -1
    )
    list1_ref[...] = there
    pltpu.make_async_copy(ghost1.at[0 : NCOL - 1], ghost1.at[0 : NCOL - 1], recv_sem.at[0]).wait()
    half = GH1 // 2
    tab1[0:128, 0:B1] = turned(ghost1[:, 0:half].reshape(B1, 128))
    tab1[0:128, B1:] = turned(ghost1[:, half:GH1].reshape(B1, 128))
    rest = turned(ghost1[:, GH1:PACK].reshape(B1, 128))
    tab1[128:D, 0:B1] = rest[0 : D - 128]
    tab1[128:D, B1:] = rest[D - 128 :]

    tab3 = turned(ghost1[:, PACK:MESSAGE].reshape(NCOL * 16, 128))
    place = iota((NCOL * 16, NOFF * B3), 0)
    low = dot(tab3, hot(place == entries3))
    high = dot(tab3[0 : D - 128], hot(place == entries3 + 8))
    found = jnp.concatenate([low, high], axis=0).astype(BF)
    for o in range(NOFF):
        g[o * D : (o + 1) * D, B1 + B2 : B1 + B2 + B3] = found[:, o * B3 : (o + 1) * B3]

    def far(o, _):
        pick = hot(iota((NCOL * GH1, B1), 0) == list1_ref[pl.ds(o, 1), :])
        at = pl.ds(pl.multiple_of(o * D, D), D)
        g[at, 0:B1] = g[at, 0:B1] + dot(tab1[...], pick).astype(BF)
        return 0

    lax.fori_loop(0, SLOTS, chunks(far, SLOTS), 0)
    far1[...] = dot(tcat[...], g[:, 0:B1])
    save = pltpu.make_async_copy(far1, out1_ref, load_sem.at[8])
    save.start()

    pltpu.make_async_copy(ghost2.at[0 : NROW - 1], ghost2.at[0 : NROW - 1], recv_sem.at[1]).wait()
    tab2 = turned(jnp.concatenate([two, ghost2[...].reshape(NROW * GH2, D)], axis=0))
    for o in range(0, NOFF, 4):
        entries = jnp.concatenate([list2[o + j : o + j + 1, :] for j in range(4)], axis=1)
        pick = hot(iota((B2 + NROW * GH2, 4 * B2), 0) == entries)
        found = dot(tab2, pick).astype(BF)
        for j in range(4):
            g[(o + j) * D : (o + j + 1) * D, B1 : B1 + B2] = found[:, j * B2 : (j + 1) * B2]

    both = dot(tcat[...], g[:, B1:]).T
    out2_ref[...] = 0.5 * both[0:B2]
    out3_ref[...] = 0.25 * both[B2 : B2 + B3]

    save.wait()
    pltpu.make_async_copy(send1.at[0 : NCOL - 1], send1.at[0 : NCOL - 1], send_sem.at[0]).wait()
    pltpu.make_async_copy(send2.at[0 : NROW - 1], send2.at[0 : NROW - 1], send_sem.at[1]).wait()


def pass_on(*refs):
    for source, target in zip(refs[0:3], refs[3:6]):
        target[...] = source[...]


def on_device(
    level_one, child_maps, translations, send_one, list_one, send_two, list_two, list_three
):
    vmem = pl.BlockSpec(memory_space=pltpu.VMEM)
    any_ = pl.BlockSpec(memory_space=pl.ANY)
    shapes = (
        jax.ShapeDtypeStruct((D, B1), F32),
        jax.ShapeDtypeStruct((B2, D), F32),
        jax.ShapeDtypeStruct((B3, D), F32),
    )
    found = pl.pallas_call(
        kernel,
        out_shape=shapes,
        in_specs=[pl.BlockSpec(memory_space=pltpu.HBM)] * 8,
        out_specs=(any_, vmem, vmem),
        scratch_shapes=[
            pltpu.VMEM((D, B1), BF),
            pltpu.VMEM((NOFF, B1), jnp.int32),
            pltpu.VMEM((8, D, D), BF),
            pltpu.VMEM((NOFF, D, D), BF),
            pltpu.VMEM((D, NOFF * D), BF),
            pltpu.VMEM((NCOL, MESSAGE, 128), BF),
            pltpu.VMEM((NCOL, MESSAGE, 128), BF),
            pltpu.VMEM((NROW, GH2, D), BF),
            pltpu.VMEM((NROW, GH2, D), BF),
            pltpu.VMEM((NOFF * D, B1 + 128), BF),
            pltpu.VMEM((D, NCOL * GH1), BF),
            pltpu.VMEM((NCOL, GH1), jnp.int32),
            pltpu.VMEM((NROW, GH2), jnp.int32),
            pltpu.VMEM((NOFF, B2), jnp.int32),
            pltpu.VMEM((B3, NOFF), jnp.int32),
            pltpu.VMEM((D, B1), F32),
            pltpu.SemaphoreType.DMA((9,)),
            pltpu.SemaphoreType.DMA((2,)),
            pltpu.SemaphoreType.DMA((2,)),
            pltpu.SemaphoreType.REGULAR,
            pltpu.SemaphoreType.REGULAR,
        ],
        compiler_params=pltpu.CompilerParams(
            collective_id=0, has_side_effects=True, vmem_limit_bytes=60 << 20
        ),
    )(
        level_one, send_one.reshape(NCOL, GH1), list_one.T, send_two.reshape(NROW, GH2),
        list_two.T, list_three, child_maps, translations,
    )
    out1, out2, out3 = pl.pallas_call(
        pass_on,
        out_shape=shapes,
        in_specs=[vmem] * 3,
        out_specs=(vmem,) * 3,
    )(*found)
    return out1, out2.T, out3.T


def solution(mesh):
    placed = (
        P(None, ("row", "col")),
        P(),
        P(),
        P(("row", "col"), None, None),
        P(("row", "col"), None),
        P(("row", "col"), None, None),
        P(("row", "col"), None),
        P(("row", "col"), None),
    )
    return jax.shard_map(
        on_device,
        mesh=mesh,
        in_specs=placed,
        out_specs=(P(None, ("row", "col")), P(None, ("row", "col")), P(None, ("row", "col"))),
        check_vma=False,
    )
```
